512 devices in a mesh: grp: 8 (over y, core), dev: 64 (over x, z).
Axes of the slice: x: 4, y: 4, z: 16, core: 2. Of those that a mesh axis runs over, the one named last changes fastest.
Arguments:
- embeddings: bfloat16 [32768, 1024], P(('grp', 'dev')), may hold values from -1000 to 1000, as said below
- labels: int32 [32768], P(('grp', 'dev')), may hold values from 0 to 2047, as said below
- order: int32 [32768], P(('grp', 'dev')), may hold values from 0 to 32767, each once
Outputs:
- max_similarity: float32 [32768], P(('grp', 'dev'))
The draws below stay inside these ranges and needn't reach their ends.
Inputs may be any that keep to these rules, and one draw needn't show every extreme that they name: On each device, at most 2 rows carry labels with one residue modulo 64; in every draw one residue has exactly 2 rows on every device. `embeddings`: rows of one cluster lie near a common direction; features and rows have unlike scales.
All inputs are finite; a program needn't handle non-finite values.
Results may differ from the reference program's by a relative error of at most 0.00059.
Values may be sent and summed in bfloat16 or wider, within the bound.
No kernel may reach another device: no remote copies, remote signals or barrier semaphores. Data moves between devices by JAX's collectives and lax.ppermute only.
A program may use at most 64 MiB of HBM per device.

```python
import math
import jax
import jax.numpy as jnp
from jax import lax

D = 1024
ROW_DEV = 64
CL_DEV = 32
CLUSTERS = 2048
CAP = 2
ROWS = 32768
N_GRP = 8
N_DEV = 64


def label_rows(key):
    hot_lane = jax.random.randint(jax.random.fold_in(key, 12), (), 0, N_DEV)
    block_count = ROWS // ROW_DEV
    block_keys = jax.random.split(jax.random.fold_in(key, 13), block_count)

    def one_block(block_key):
        slot_key, shuffle_key, pick_key = jax.random.split(block_key, 3)
        others = jax.random.permutation(slot_key, (N_DEV - 1) * CAP)[:ROW_DEV - CAP]
        lane_ids = others // CAP
        lane_ids = lane_ids + (lane_ids >= hot_lane).astype(jnp.int32)
        target = jnp.concatenate([jnp.full((CAP,), hot_lane, jnp.int32), lane_ids.astype(jnp.int32)])
        target = jax.random.permutation(shuffle_key, target)
        picks = jnp.min(jax.random.randint(pick_key, (3, ROW_DEV), 0, CL_DEV), axis=0)
        return (target + N_DEV * picks).astype(jnp.int32)
    return jax.vmap(one_block)(block_keys).reshape(ROWS)


def draw_labels(key, part):
    return label_rows(key)


def draw_embeddings(key, part):
    cluster_ids = label_rows(key)
    key = jax.random.fold_in(key, 21)
    centre_key, noise_key, row_key, feature_key = jax.random.split(key, 4)
    centres = jax.random.normal(centre_key, (CLUSTERS, D), jnp.float32)
    row_scale = jnp.exp(jax.random.uniform(row_key, (ROWS, 1), jnp.float32, 0.0, math.log(10.0)))
    feature_scale = jnp.exp(jax.random.uniform(feature_key, (1, D), jnp.float32, 0.0, math.log(10.0)))
    noise = jax.random.normal(noise_key, (ROWS, D), jnp.float32)
    mixed = 0.7 * centres[cluster_ids] + noise
    mixed = jnp.clip(mixed, -9.0, 9.0)
    return (row_scale * feature_scale * mixed).astype(jnp.bfloat16)


def setup_inputs(seed: int = 0) -> dict:
    keys = jax.random.split(jax.random.key(seed), 4)
    embeddings = draw_embeddings(jax.random.fold_in(keys[3], 71), 0)
    labels = draw_labels(jax.random.fold_in(keys[3], 71), 0)
    order = jax.random.permutation(keys[2], ROWS).astype(jnp.int32)
    return dict(embeddings=embeddings, labels=labels, order=order)


EPSILON = 1e-06

def reference(embeddings, labels, order):
    floats = embeddings.astype(jnp.float32)
    unit_rows = (floats * lax.rsqrt(lax.optimization_barrier(jnp.sum(floats * floats, axis=1, keepdims=True)) + D * EPSILON)).astype(jnp.bfloat16)
    owners = (labels % N_DEV).astype(jnp.int32)
    sorted_rows = jnp.argsort(owners, stable=True).astype(jnp.int32)
    counts = lax.optimization_barrier(jnp.sum((owners[:, None] == jnp.arange(N_DEV, dtype=jnp.int32)[None, :]).astype(jnp.int32), axis=0))
    starts = (jnp.cumsum(counts) - counts).astype(jnp.int32)
    column_rows = 2 * ROW_DEV * N_GRP
    padded = jnp.concatenate([sorted_rows, jnp.zeros((column_rows,), jnp.int32)])

    def column(lane_index):
        taken = lax.dynamic_slice(padded, (starts[lane_index],), (column_rows,))
        live_slot = jnp.arange(column_rows, dtype=jnp.int32) < counts[lane_index]
        member_rows = unit_rows[taken]
        member_labels = jnp.where(live_slot, labels[taken], -1)
        member_order = order[taken]
        scores = jnp.dot(member_rows, member_rows.T, preferred_element_type=jnp.float32)
        valid = (member_labels[:, None] == member_labels[None, :]) & (member_labels[None, :] >= 0)
        valid = valid & (member_order[None, :] < member_order[:, None])
        best_score = lax.optimization_barrier(jnp.max(jnp.where(valid, scores, -1.0), axis=1))
        return (jnp.where(live_slot, best_score, -2.0), taken)
    best_all, taken_all = lax.map(column, jnp.arange(N_DEV, dtype=jnp.int32))
    result = jnp.full((ROWS,), -2.0, jnp.float32)
    return result.at[taken_all.reshape(-1)].max(best_all.reshape(-1))
```

```python
import jax
import jax.numpy as jnp
from jax import lax
from jax.experimental import pallas as pl
from jax.experimental.pallas import tpu as pltpu
from jax.sharding import PartitionSpec as P

EPSILON = 1e-06
NX = 4
META = 128
NT = (((1,), (1,)), ((), ()))
VMEM = pl.BlockSpec(memory_space=pltpu.VMEM)


def slots(labels, lanes):
    rows = labels.shape[1]
    target = lax.rem(labels, lanes)
    hit = lax.broadcasted_iota(jnp.int32, (lanes, rows), 0) == target
    earlier = lax.broadcasted_iota(jnp.int32, (rows, rows), 0) < lax.broadcasted_iota(jnp.int32, (rows, rows), 1)
    before = jnp.dot(
        hit.astype(jnp.bfloat16), earlier.astype(jnp.bfloat16), preferred_element_type=jnp.float32
    )
    place = jnp.sum(jnp.where(hit, before, 0.0), axis=0, keepdims=True).astype(jnp.int32)
    return target, hit, place


def pack_kernel(lanes, emb_ref, labels_ref, order_ref, out_ref):
    rows, width = emb_ref.shape
    slot_count = out_ref.shape[0]
    floats = emb_ref[...].astype(jnp.float32)
    scale = lax.rsqrt(jnp.sum(floats * floats, axis=1, keepdims=True) + width * EPSILON)
    unit = (floats * scale).astype(jnp.bfloat16)
    labels = labels_ref[...]
    target, _, place = slots(labels, lanes)
    cap = slot_count // lanes
    here = lax.broadcasted_iota(jnp.int32, (slot_count, rows), 0) == target * cap + place
    out_ref[:, :width] = jnp.dot(
        here.astype(jnp.bfloat16), unit, preferred_element_type=jnp.float32
    ).astype(jnp.bfloat16)

    def column(values):
        return jnp.sum(jnp.where(here, values.astype(jnp.float32), 0.0), axis=1, keepdims=True)

    order = order_ref[...]
    lane = lax.broadcasted_iota(jnp.int32, (slot_count, META), 1)
    meta = jnp.where(lane == 0, column(labels // lanes + 1), 0.0)
    meta = jnp.where(lane == 1, column(order // 256), meta)
    meta = jnp.where(lane == 2, column(lax.rem(order, 256)), meta)
    out_ref[:, width:] = meta.astype(jnp.bfloat16)


def gram_kernel(a_ref, b_ref, c_ref, d_ref, *outs):
    width = a_ref.shape[1] - META
    size = a_ref.shape[0]
    blocks = jnp.concatenate([a_ref[...], b_ref[...], c_ref[...], d_ref[...]], axis=0)
    keys, meta = blocks[:, :width], blocks[:, width:]
    scores = lax.dot_general(keys, keys, NT, preferred_element_type=jnp.float32)
    r = lax.broadcasted_iota(jnp.int32, (8, META), 0)
    c = lax.broadcasted_iota(jnp.int32, (8, META), 1)
    weights = jnp.where((r == 0) & (c == 0) | (r == 1) & (c == 2), 1.0, 0.0)
    weights = jnp.where((r == 1) & (c == 1), 256.0, weights).astype(jnp.bfloat16)
    across = lax.dot_general(weights, meta, NT, preferred_element_type=jnp.float32)
    down = meta[:, :8].astype(jnp.float32)
    label_down = down[:, 0:1]
    order_down = down[:, 1:2] * 256.0 + down[:, 2:3]
    valid = (label_down == across[0:1, :]) & (order_down < across[1:2, :])
    best = jnp.max(jnp.where(valid, scores, -1.0), axis=0, keepdims=True)
    for k, out in enumerate(outs):
        out[...] = best[:, k * size : (k + 1) * size]


def spread_kernel(nz, a_ref, b_ref, c_ref, d_ref, out_ref):
    best = jnp.maximum(jnp.maximum(a_ref[...], b_ref[...]), jnp.maximum(c_ref[...], d_ref[...]))
    lanes, size = out_ref.shape
    cap = size // lanes
    home = lax.broadcasted_iota(jnp.int32, (lanes, size), 0)
    slot = lax.broadcasted_iota(jnp.int32, (lanes, size), 1) // cap
    mine = home == lax.rem(slot, NX) * nz + slot // NX
    out_ref[...] = jnp.where(mine, best, -4.0)


def pick_kernel(returned_ref, labels_ref, out_ref):
    lanes, size = returned_ref.shape
    _, hit, place = slots(labels_ref[...], lanes)
    cap = size // lanes
    lane = lax.rem(lax.broadcasted_iota(jnp.int32, (lanes, size), 1), cap)
    returned = returned_ref[...]
    best = jnp.full(hit.shape, -4.0, jnp.float32)
    for p in range(cap):
        value = jnp.max(jnp.where(lane == p, returned, -4.0), axis=1, keepdims=True)
        best = jnp.where(hit & (place == p), value, best)
    out_ref[...] = jnp.max(best, axis=0, keepdims=True)


def call(kernel, outs, count):
    return pl.pallas_call(
        kernel,
        out_shape=outs,
        in_specs=[VMEM] * count,
        out_specs=jax.tree.map(lambda _: VMEM, outs),
        compiler_params=pltpu.CompilerParams(vmem_limit_bytes=16 * 1024 * 1024),
    )


def body(embeddings, labels, order):
    rows, width = embeddings.shape
    lanes = lax.axis_size("dev")
    groups = lax.axis_size("grp")
    nz = lanes // NX
    cap = 2 * rows // lanes
    slot_count = lanes * cap
    wide = width + META
    labels, order = labels.reshape(1, rows), order.reshape(1, rows)
    along_x = [[x * nz + z for x in range(NX)] for z in range(nz)]
    along_z = [[x * nz + z for z in range(nz)] for x in range(NX)]

    sent = call(
        lambda *refs: pack_kernel(lanes, *refs), jax.ShapeDtypeStruct((slot_count, wide), jnp.bfloat16), 3
    )(embeddings, labels, order)
    sent = lax.all_to_all(
        sent.reshape(NX, nz * cap, wide), "dev", 0, 0, axis_index_groups=along_x, tiled=True
    )
    sent = sent.reshape(NX, nz, cap, wide).transpose(1, 0, 2, 3).reshape(nz, NX * cap, wide)
    sent = lax.all_to_all(sent, "dev", 0, 0, axis_index_groups=along_z, tiled=True)
    block = sent.reshape(slot_count, wide)

    def moves(shift, flip):
        return [(i, (i + shift) % groups ^ flip) for i in range(groups)]

    steps = [moves(groups // 2, 1), moves(2, 0), moves(0, 1)]
    fetched = [lax.ppermute(block, "grp", step) for step in steps]
    partial = call(gram_kernel, [jax.ShapeDtypeStruct((1, slot_count), jnp.float32)] * 4, 4)(block, *fetched)
    back = [
        lax.ppermute(part, "grp", [(j, i) for i, j in step]) for part, step in zip(partial[1:], steps)
    ]
    spread = call(
        lambda *refs: spread_kernel(nz, *refs), jax.ShapeDtypeStruct((lanes, slot_count), jnp.float32), 4
    )(partial[0], *back)
    returned = lax.all_to_all(spread.reshape(lanes, 1, slot_count), "dev", 0, 0, tiled=True)
    best = call(pick_kernel, jax.ShapeDtypeStruct((1, rows), jnp.float32), 2)(
        returned.reshape(lanes, slot_count), labels
    )
    return best.reshape(rows)


def solution(mesh):
    placed = (P(("grp", "dev"), None), P(("grp", "dev")), P(("grp", "dev")))
    return jax.shard_map(
        body, mesh=mesh, in_specs=placed, out_specs=P(("grp", "dev")), check_vma=False
    )
```

```python
import jax
import jax.numpy as jnp
from jax import lax
from jax.experimental import pallas as pl
from jax.experimental.pallas import tpu as pltpu
from jax.sharding import Mesh
from jax.sharding import PartitionSpec as P

EPSILON = 1e-06
NX = 4
NY = 4
META = 128
NT = (((1,), (1,)), ((), ()))
VMEM = pl.BlockSpec(memory_space=pltpu.VMEM)


def slots(labels, lanes):
    rows = labels.shape[1]
    target = lax.rem(labels, lanes)
    hit = lax.broadcasted_iota(jnp.int32, (lanes, rows), 0) == target
    earlier = lax.broadcasted_iota(jnp.int32, (rows, rows), 0) < lax.broadcasted_iota(jnp.int32, (rows, rows), 1)
    before = jnp.dot(
        hit.astype(jnp.bfloat16), earlier.astype(jnp.bfloat16), preferred_element_type=jnp.float32
    )
    place = jnp.sum(jnp.where(hit, before, 0.0), axis=0, keepdims=True).astype(jnp.int32)
    return target, hit, place


def pack_kernel(lanes, emb_ref, labels_ref, order_ref, out_ref):
    rows, width = emb_ref.shape
    slot_count = out_ref.shape[0]
    floats = emb_ref[...].astype(jnp.float32)
    scale = lax.rsqrt(jnp.sum(floats * floats, axis=1, keepdims=True) + width * EPSILON)
    unit = (floats * scale).astype(jnp.bfloat16)
    labels = labels_ref[...]
    target, _, place = slots(labels, lanes)
    cap = slot_count // lanes
    here = lax.broadcasted_iota(jnp.int32, (slot_count, rows), 0) == target * cap + place
    out_ref[:, :width] = jnp.dot(
        here.astype(jnp.bfloat16), unit, preferred_element_type=jnp.float32
    ).astype(jnp.bfloat16)

    def column(values):
        return jnp.sum(jnp.where(here, values.astype(jnp.float32), 0.0), axis=1, keepdims=True)

    order = order_ref[...]
    lane = lax.broadcasted_iota(jnp.int32, (slot_count, META), 1)
    meta = jnp.where(lane == 0, column(labels // lanes + 1), 0.0)
    meta = jnp.where(lane == 1, column(order // 256), meta)
    meta = jnp.where(lane == 2, column(lax.rem(order, 256)), meta)
    out_ref[:, width:] = meta.astype(jnp.bfloat16)


def gram_kernel(core_ref, own_ref, other_ref, lane_ref, out_ref):
    width = own_ref.shape[1] - META
    size = own_ref.shape[0]
    dests = out_ref.shape[0] // 2
    core = core_ref[0]
    queries = jnp.concatenate([own_ref[...], other_ref[...]], axis=0)
    members = lane_ref[...]
    scores = lax.dot_general(
        members[:, :width], queries[:, :width], NT, preferred_element_type=jnp.float32
    )
    r = lax.broadcasted_iota(jnp.int32, (8, META), 0)
    c = lax.broadcasted_iota(jnp.int32, (8, META), 1)
    weights = jnp.where((r == 0) & (c == 0) | (r == 1) & (c == 2), 1.0, 0.0)
    weights = jnp.where((r == 1) & (c == 1), 256.0, weights).astype(jnp.bfloat16)
    across = lax.dot_general(weights, queries[:, width:], NT, preferred_element_type=jnp.float32)
    down = members[:, width:].astype(jnp.float32)
    label_down = down[:, 0:1]
    order_down = down[:, 1:2] * 256.0 + down[:, 2:3]
    valid = (label_down == across[0:1, :]) & (order_down < across[1:2, :])
    best = jnp.max(jnp.where(valid, scores, -1.0), axis=0, keepdims=True)
    own, other = best[:, :size], best[:, size:]
    home = lax.broadcasted_iota(jnp.int32, (dests, size), 0)
    slot = lax.broadcasted_iota(jnp.int32, (dests, size), 1) // (size // dests)
    mine = home == slot
    out_ref[:dests, :] = jnp.where(mine, jnp.where(core == 0, own, other), -4.0)
    out_ref[dests:, :] = jnp.where(mine, jnp.where(core == 0, other, own), -4.0)


def pick_kernel(returned_ref, labels_ref, out_ref):
    lanes, size = returned_ref.shape[0] // 2, returned_ref.shape[1]
    _, hit, place = slots(labels_ref[...], lanes)
    cap = size // lanes
    lane = lax.rem(lax.broadcasted_iota(jnp.int32, (lanes, size), 1), cap)
    returned = jnp.maximum(returned_ref[:lanes, :], returned_ref[lanes:, :])
    best = jnp.full(hit.shape, -4.0, jnp.float32)
    for p in range(cap):
        value = jnp.max(jnp.where(lane == p, returned, -4.0), axis=1, keepdims=True)
        best = jnp.where(hit & (place == p), value, best)
    out_ref[...] = jnp.max(best, axis=0, keepdims=True)


def call(kernel, outs, specs):
    return pl.pallas_call(
        kernel,
        out_shape=outs,
        in_specs=specs,
        out_specs=jax.tree.map(lambda _: VMEM, outs),
        compiler_params=pltpu.CompilerParams(vmem_limit_bytes=16 * 1024 * 1024),
    )


def body(embeddings, labels, order):
    rows, width = embeddings.shape
    lanes = lax.axis_size(("x", "z"))
    cap = 2 * rows // lanes
    slot_count = lanes * cap
    wide = width + META
    labels, order = labels.reshape(1, rows), order.reshape(1, rows)

    sent = call(
        lambda *refs: pack_kernel(lanes, *refs),
        jax.ShapeDtypeStruct((slot_count, wide), jnp.bfloat16),
        [VMEM] * 3,
    )(embeddings, labels, order)
    block = lax.all_to_all(sent.reshape(lanes, cap, wide), ("x", "z"), 0, 0, tiled=True)
    block = block.reshape(slot_count, wide)

    other = lax.ppermute(block, "core", [(0, 1), (1, 0)])
    copies = jnp.broadcast_to(block[None], (NY, slot_count, wide))
    lane = lax.all_to_all(copies, "y", 0, 0, tiled=True).reshape(NY * slot_count, wide)
    core = lax.axis_index("core").astype(jnp.int32).reshape(1)
    partial = call(
        gram_kernel,
        jax.ShapeDtypeStruct((2 * lanes, slot_count), jnp.float32),
        [pl.BlockSpec(memory_space=pltpu.SMEM)] + [VMEM] * 3,
    )(core, block, other, lane)
    returned = lax.all_to_all(
        partial.reshape(2 * lanes, 1, slot_count), ("core", "x", "z"), 0, 0, tiled=True
    )
    best = call(pick_kernel, jax.ShapeDtypeStruct((1, rows), jnp.float32), [VMEM] * 2)(
        returned.reshape(2 * lanes, slot_count), labels
    )
    return best.reshape(rows)


def solution(mesh):
    axes = ("y", "core", "x", "z")
    chips = Mesh(mesh.devices.reshape(NY, 2, NX, -1), axes)
    placed = (P(axes, None), P(axes), P(axes))
    return jax.shard_map(body, mesh=chips, in_specs=placed, out_specs=P(axes), check_vma=False)
```

```python
import jax
import jax.numpy as jnp
from jax import lax
from jax.experimental import pallas as pl
from jax.experimental.pallas import tpu as pltpu
from jax.sharding import Mesh
from jax.sharding import PartitionSpec as P

EPSILON = 1e-06
NX = 4
NY = 4
META = 128
NT = (((1,), (1,)), ((), ()))
VMEM = pl.BlockSpec(memory_space=pltpu.VMEM)


def slots(labels, lanes):
    rows = labels.shape[1]
    target = lax.rem(labels, lanes)
    hit = lax.broadcasted_iota(jnp.int32, (lanes, rows), 0) == target
    earlier = lax.broadcasted_iota(jnp.int32, (rows, rows), 0) < lax.broadcasted_iota(jnp.int32, (rows, rows), 1)
    before = jnp.dot(
        hit.astype(jnp.bfloat16), earlier.astype(jnp.bfloat16), preferred_element_type=jnp.float32
    )
    place = jnp.sum(jnp.where(hit, before, 0.0), axis=0, keepdims=True).astype(jnp.int32)
    return target, hit, place


def pack_kernel(lanes, emb_hbm, labels_hbm, order_hbm, out_ref, emb_ref, labels_ref, order_ref, arrived):
    copies = [
        pltpu.make_async_copy(source, target, arrived.at[k])
        for k, (source, target) in enumerate(
            [(emb_hbm, emb_ref), (labels_hbm, labels_ref), (order_hbm, order_ref)]
        )
    ]
    for copy in copies:
        copy.start()
    for copy in copies:
        copy.wait()
    rows, width = emb_ref.shape
    slot_count = out_ref.shape[0]
    floats = emb_ref[...].astype(jnp.float32)
    scale = lax.rsqrt(jnp.sum(floats * floats, axis=1, keepdims=True) + width * EPSILON)
    unit = (floats * scale).astype(jnp.bfloat16)
    labels = labels_ref[...]
    target, _, place = slots(labels, lanes)
    cap = slot_count // lanes
    here = lax.broadcasted_iota(jnp.int32, (slot_count, rows), 0) == target * cap + place
    out_ref[:, :width] = jnp.dot(
        here.astype(jnp.bfloat16), unit, preferred_element_type=jnp.float32
    ).astype(jnp.bfloat16)

    def column(values):
        return jnp.sum(jnp.where(here, values.astype(jnp.float32), 0.0), axis=1, keepdims=True)

    order = order_ref[...]
    lane = lax.broadcasted_iota(jnp.int32, (slot_count, META), 1)
    meta = jnp.where(lane == 0, column(labels // lanes + 1), 0.0)
    meta = jnp.where(lane == 1, column(order // 256), meta)
    meta = jnp.where(lane == 2, column(lax.rem(order, 256)), meta)
    out_ref[:, width:] = meta.astype(jnp.bfloat16)


def copies_kernel(block_ref, out_ref):
    for k in range(out_ref.shape[0]):
        out_ref[k] = block_ref[...]


def gram_kernel(own_ref, other_ref, lane_ref, own_out, other_out):
    width = own_ref.shape[1] - META
    size = own_ref.shape[0]
    queries = jnp.concatenate([own_ref[...], other_ref[...]], axis=0)
    members = lane_ref[...]
    scores = lax.dot_general(
        members[:, :width], queries[:, :width], NT, preferred_element_type=jnp.float32
    )
    r = lax.broadcasted_iota(jnp.int32, (8, META), 0)
    c = lax.broadcasted_iota(jnp.int32, (8, META), 1)
    weights = jnp.where((r == 0) & (c == 0) | (r == 1) & (c == 2), 1.0, 0.0)
    weights = jnp.where((r == 1) & (c == 1), 256.0, weights).astype(jnp.bfloat16)
    across = lax.dot_general(weights, queries[:, width:], NT, preferred_element_type=jnp.float32)
    down = members[:, width:].astype(jnp.float32)
    label_down = down[:, 0:1]
    order_down = down[:, 1:2] * 256.0 + down[:, 2:3]
    valid = (label_down == across[0:1, :]) & (order_down < across[1:2, :])
    best = jnp.max(jnp.where(valid, scores, -1.0), axis=0, keepdims=True)
    own_out[...] = best[:, :size]
    other_out[...] = best[:, size:]


def spread_kernel(own_ref, back_ref, out_ref):
    dests, size = out_ref.shape
    best = jnp.maximum(own_ref[...], back_ref[...])
    home = lax.broadcasted_iota(jnp.int32, (dests, size), 0)
    slot = lax.broadcasted_iota(jnp.int32, (dests, size), 1) // (size // dests)
    out_ref[...] = jnp.where(home == slot, best, -4.0)


def pick_kernel(returned_ref, labels_ref, out_ref):
    lanes, size = returned_ref.shape
    _, hit, place = slots(labels_ref[...], lanes)
    cap = size // lanes
    lane = lax.rem(lax.broadcasted_iota(jnp.int32, (lanes, size), 1), cap)
    returned = returned_ref[...]
    best = jnp.full(hit.shape, -4.0, jnp.float32)
    for p in range(cap):
        value = jnp.max(jnp.where(lane == p, returned, -4.0), axis=1, keepdims=True)
        best = jnp.where(hit & (place == p), value, best)
    out_ref[...] = jnp.max(best, axis=0, keepdims=True)


def call(kernel, outs, specs, scratch=()):
    return pl.pallas_call(
        kernel,
        out_shape=outs,
        in_specs=specs,
        out_specs=jax.tree.map(lambda _: VMEM, outs),
        scratch_shapes=scratch,
        compiler_params=pltpu.CompilerParams(vmem_limit_bytes=16 * 1024 * 1024),
    )


def body(embeddings, labels, order):
    rows, width = embeddings.shape
    lanes = lax.axis_size(("x", "z"))
    cap = 2 * rows // lanes
    slot_count = lanes * cap
    wide = width + META
    labels, order = labels.reshape(1, rows), order.reshape(1, rows)

    sent = call(
        lambda *refs: pack_kernel(lanes, *refs),
        jax.ShapeDtypeStruct((slot_count, wide), jnp.bfloat16),
        [pl.BlockSpec(memory_space=pltpu.HBM)] * 3,
        [
            pltpu.VMEM((rows, width), jnp.bfloat16),
            pltpu.VMEM((1, rows), jnp.int32),
            pltpu.VMEM((1, rows), jnp.int32),
            pltpu.SemaphoreType.DMA((3,)),
        ],
    )(embeddings, labels, order)
    block = lax.all_to_all(sent.reshape(lanes, cap, wide), ("x", "z"), 0, 0, tiled=True)
    block = block.reshape(slot_count, wide)

    swap = [(0, 1), (1, 0)]
    other = lax.ppermute(block, "core", swap)
    copies = call(
        copies_kernel, jax.ShapeDtypeStruct((NY, slot_count, wide), jnp.bfloat16), [VMEM]
    )(block)
    lane = lax.all_to_all(copies, "y", 0, 0, tiled=True).reshape(NY * slot_count, wide)
    own_best, other_best = call(
        gram_kernel, [jax.ShapeDtypeStruct((1, slot_count), jnp.float32)] * 2, [VMEM] * 3
    )(block, other, lane)
    spread = call(
        spread_kernel, jax.ShapeDtypeStruct((lanes, slot_count), jnp.float32), [VMEM] * 2
    )(own_best, lax.ppermute(other_best, "core", swap))
    returned = lax.all_to_all(spread.reshape(lanes, 1, slot_count), ("x", "z"), 0, 0, tiled=True)
    best = call(pick_kernel, jax.ShapeDtypeStruct((1, rows), jnp.float32), [VMEM] * 2)(
        returned.reshape(lanes, slot_count), labels
    )
    return best.reshape(rows)


def solution(mesh):
    axes = ("y", "core", "x", "z")
    chips = Mesh(mesh.devices.reshape(NY, 2, NX, -1), axes)
    placed = (P(axes, None), P(axes), P(axes))
    return jax.shard_map(body, mesh=chips, in_specs=placed, out_specs=P(axes), check_vma=False)
```

```python
import jax
import jax.numpy as jnp
from jax import lax
from jax.experimental import pallas as pl
from jax.experimental.pallas import tpu as pltpu
from jax.sharding import Mesh
from jax.sharding import PartitionSpec as P

EPSILON = 1e-06
NX = 4
NY = 4
META = 128
NT = (((1,), (1,)), ((), ()))
VMEM = pl.BlockSpec(memory_space=pltpu.VMEM)


def slots(labels, lanes):
    rows = labels.shape[1]
    target = lax.rem(labels, lanes)
    hit = lax.broadcasted_iota(jnp.int32, (lanes, rows), 0) == target
    earlier = lax.broadcasted_iota(jnp.int32, (rows, rows), 0) < lax.broadcasted_iota(jnp.int32, (rows, rows), 1)
    before = jnp.dot(
        hit.astype(jnp.bfloat16), earlier.astype(jnp.bfloat16), preferred_element_type=jnp.float32
    )
    place = jnp.sum(jnp.where(hit, before, 0.0), axis=0, keepdims=True).astype(jnp.int32)
    return target, hit, place


def pack_kernel(lanes, emb_hbm, labels_hbm, order_hbm, out_ref, emb_ref, labels_ref, order_ref, arrived):
    parts = [(labels_hbm, labels_ref), (order_hbm, order_ref), (emb_hbm, emb_ref)]
    copies = [
        pltpu.make_async_copy(source, target, arrived.at[k]) for k, (source, target) in enumerate(parts)
    ]
    for copy in copies:
        copy.start()
    rows, width = emb_ref.shape
    slot_count = out_ref.shape[0]
    copies[0].wait()
    copies[1].wait()
    labels, order = labels_ref[...], order_ref[...]
    target, _, place = slots(labels, lanes)
    cap = slot_count // lanes
    here = lax.broadcasted_iota(jnp.int32, (slot_count, rows), 0) == target * cap + place

    def column(values):
        return jnp.sum(jnp.where(here, values.astype(jnp.float32), 0.0), axis=1, keepdims=True)

    lane = lax.broadcasted_iota(jnp.int32, (slot_count, META), 1)
    meta = jnp.where(lane == 0, column(labels // lanes + 1), 0.0)
    meta = jnp.where(lane == 1, column(order // 256), meta)
    meta = jnp.where(lane == 2, column(lax.rem(order, 256)), meta)
    out_ref[:, width:] = meta.astype(jnp.bfloat16)

    copies[2].wait()
    floats = emb_ref[...].astype(jnp.float32)
    scale = lax.rsqrt(jnp.sum(floats * floats, axis=1, keepdims=True) + width * EPSILON)
    unit = (floats * scale).astype(jnp.bfloat16)
    out_ref[:, :width] = jnp.dot(
        here.astype(jnp.bfloat16), unit, preferred_element_type=jnp.float32
    ).astype(jnp.bfloat16)


def gram_kernel(core_ref, own_ref, other_ref, lane_ref, out_ref):
    width = own_ref.shape[1] - META
    size = own_ref.shape[0]
    dests = out_ref.shape[0] // 2
    core = core_ref[0]
    queries = jnp.concatenate([own_ref[...], other_ref[...]], axis=0)
    members = lane_ref[...]
    scores = lax.dot_general(
        members[:, :width], queries[:, :width], NT, preferred_element_type=jnp.float32
    )
    r = lax.broadcasted_iota(jnp.int32, (8, META), 0)
    c = lax.broadcasted_iota(jnp.int32, (8, META), 1)
    weights = jnp.where((r == 0) & (c == 0) | (r == 1) & (c == 2), 1.0, 0.0)
    weights = jnp.where((r == 1) & (c == 1), 256.0, weights).astype(jnp.bfloat16)
    across = lax.dot_general(weights, queries[:, width:], NT, preferred_element_type=jnp.float32)
    down = members[:, width:].astype(jnp.float32)
    label_down = down[:, 0:1]
    order_down = down[:, 1:2] * 256.0 + down[:, 2:3]
    valid = (label_down == across[0:1, :]) & (order_down < across[1:2, :])
    best = jnp.max(jnp.where(valid, scores, -1.0), axis=0, keepdims=True)
    own, other = best[:, :size], best[:, size:]
    home = lax.broadcasted_iota(jnp.int32, (dests, size), 0)
    slot = lax.broadcasted_iota(jnp.int32, (dests, size), 1) // (size // dests)
    mine = home == slot
    out_ref[:dests, :] = jnp.where(mine, jnp.where(core == 0, own, other), -4.0)
    out_ref[dests:, :] = jnp.where(mine, jnp.where(core == 0, other, own), -4.0)


def pick_kernel(returned_ref, labels_ref, out_ref):
    lanes, size = returned_ref.shape[0] // 2, returned_ref.shape[1]
    _, hit, place = slots(labels_ref[...], lanes)
    cap = size // lanes
    lane = lax.rem(lax.broadcasted_iota(jnp.int32, (lanes, size), 1), cap)
    returned = jnp.maximum(returned_ref[:lanes, :], returned_ref[lanes:, :])
    best = jnp.full(hit.shape, -4.0, jnp.float32)
    for p in range(cap):
        value = jnp.max(jnp.where(lane == p, returned, -4.0), axis=1, keepdims=True)
        best = jnp.where(hit & (place == p), value, best)
    out_ref[...] = jnp.max(best, axis=0, keepdims=True)


def call(kernel, outs, specs, scratch=()):
    return pl.pallas_call(
        kernel,
        out_shape=outs,
        in_specs=specs,
        out_specs=jax.tree.map(lambda _: VMEM, outs),
        scratch_shapes=scratch,
        compiler_params=pltpu.CompilerParams(vmem_limit_bytes=16 * 1024 * 1024),
    )


def body(embeddings, labels, order):
    rows, width = embeddings.shape
    lanes = lax.axis_size(("x", "z"))
    cap = 2 * rows // lanes
    slot_count = lanes * cap
    wide = width + META
    labels, order = labels.reshape(1, rows), order.reshape(1, rows)

    sent = call(
        lambda *refs: pack_kernel(lanes, *refs),
        jax.ShapeDtypeStruct((slot_count, wide), jnp.bfloat16),
        [pl.BlockSpec(memory_space=pltpu.HBM)] * 3,
        [
            pltpu.VMEM((rows, width), jnp.bfloat16),
            pltpu.VMEM((1, rows), jnp.int32),
            pltpu.VMEM((1, rows), jnp.int32),
            pltpu.SemaphoreType.DMA((3,)),
        ],
    )(*[pltpu.with_memory_space_constraint(a, pltpu.HBM) for a in (embeddings, labels, order)])
    block = lax.all_to_all(sent.reshape(lanes, cap, wide), ("x", "z"), 0, 0, tiled=True)
    block = block.reshape(slot_count, wide)

    other = lax.ppermute(block, "core", [(0, 1), (1, 0)])
    copies = jnp.broadcast_to(block[None], (NY, slot_count, wide))
    lane = lax.all_to_all(copies, "y", 0, 0, tiled=True).reshape(NY * slot_count, wide)
    core = lax.axis_index("core").astype(jnp.int32).reshape(1)
    partial = call(
        gram_kernel,
        jax.ShapeDtypeStruct((2 * lanes, slot_count), jnp.float32),
        [pl.BlockSpec(memory_space=pltpu.SMEM)] + [VMEM] * 3,
    )(core, block, other, lane)
    returned = lax.all_to_all(
        partial.reshape(2 * lanes, 1, slot_count), ("core", "x", "z"), 0, 0, tiled=True
    )
    best = call(pick_kernel, jax.ShapeDtypeStruct((1, rows), jnp.float32), [VMEM] * 2)(
        returned.reshape(2 * lanes, slot_count), labels
    )
    return best.reshape(rows)


def solution(mesh):
    axes = ("y", "core", "x", "z")
    chips = Mesh(mesh.devices.reshape(NY, 2, NX, -1), axes)
    placed = (P(axes, None), P(axes), P(axes))
    return jax.shard_map(body, mesh=chips, in_specs=placed, out_specs=P(axes), check_vma=False)
```

```python
import jax
import jax.numpy as jnp
from jax import lax
from jax.experimental import pallas as pl
from jax.experimental.pallas import tpu as pltpu
from jax.sharding import Mesh
from jax.sharding import PartitionSpec as P

EPSILON = 1e-06
DOWN, ACROSS = 4, 4
SERIAL = 7
NX = 4
NY = 4
META = 128
NT = (((1,), (1,)), ((), ()))
VMEM = pl.BlockSpec(memory_space=pltpu.VMEM)


def slots(labels, lanes):
    rows = labels.shape[1]
    target = lax.rem(labels, lanes)
    hit = lax.broadcasted_iota(jnp.int32, (lanes, rows), 0) == target
    earlier = lax.broadcasted_iota(jnp.int32, (rows, rows), 0) < lax.broadcasted_iota(jnp.int32, (rows, rows), 1)
    before = jnp.dot(
        hit.astype(jnp.bfloat16), earlier.astype(jnp.bfloat16), preferred_element_type=jnp.float32
    )
    place = jnp.sum(jnp.where(hit, before, 0.0), axis=0, keepdims=True).astype(jnp.int32)
    return target, hit, place


def pack_kernel(lanes, core_ref, emb_hbm, labels_hbm, order_hbm, out_ref, emb_ref, labels_ref, order_ref, arrived):
    rows, width = emb_ref.shape
    tall, wide = rows // DOWN, width // ACROSS
    pieces = [(pl.ds(r * tall, tall), pl.ds(c * wide, wide)) for r in range(DOWN) for c in range(ACROSS)]
    parts = [(labels_hbm, labels_ref), (order_hbm, order_ref)]
    parts += [(emb_hbm.at[piece], emb_ref.at[piece]) for piece in pieces]
    copies = [
        pltpu.make_async_copy(source, target, arrived.at[k]) for k, (source, target) in enumerate(parts)
    ]
    paced, others = copies[2 : 2 + SERIAL], copies[2 + SERIAL :]
    goes_first = core_ref[0] == 1
    for copy in copies[:2]:
        copy.start()
    for copy in paced:
        copy.start()

        @pl.when(jnp.logical_not(goes_first))
        def _():
            copy.wait()

    for copy in others:
        copy.start()

    slot_count = out_ref.shape[0]
    copies[0].wait()
    copies[1].wait()
    labels, order = labels_ref[...], order_ref[...]
    target, _, place = slots(labels, lanes)
    cap = slot_count // lanes
    here = lax.broadcasted_iota(jnp.int32, (slot_count, rows), 0) == target * cap + place

    def column(values):
        return jnp.sum(jnp.where(here, values.astype(jnp.float32), 0.0), axis=1, keepdims=True)

    lane = lax.broadcasted_iota(jnp.int32, (slot_count, META), 1)
    meta = jnp.where(lane == 0, column(labels // lanes + 1), 0.0)
    meta = jnp.where(lane == 1, column(order // 256), meta)
    meta = jnp.where(lane == 2, column(lax.rem(order, 256)), meta)
    out_ref[:, width:] = meta.astype(jnp.bfloat16)

    for copy in others:
        copy.wait()

    @pl.when(goes_first)
    def _():
        for copy in paced:
            copy.wait()

    floats = emb_ref[...].astype(jnp.float32)
    scale = lax.rsqrt(jnp.sum(floats * floats, axis=1, keepdims=True) + width * EPSILON)
    unit = (floats * scale).astype(jnp.bfloat16)
    out_ref[:, :width] = jnp.dot(
        here.astype(jnp.bfloat16), unit, preferred_element_type=jnp.float32
    ).astype(jnp.bfloat16)


def gram_kernel(core_ref, own_ref, other_ref, lane_ref, out_ref):
    width = own_ref.shape[1] - META
    size = own_ref.shape[0]
    dests = out_ref.shape[0] // 2
    core = core_ref[0]
    queries = jnp.concatenate([own_ref[...], other_ref[...]], axis=0)
    members = lane_ref[...]
    scores = lax.dot_general(
        members[:, :width], queries[:, :width], NT, preferred_element_type=jnp.float32
    )
    r = lax.broadcasted_iota(jnp.int32, (8, META), 0)
    c = lax.broadcasted_iota(jnp.int32, (8, META), 1)
    weights = jnp.where((r == 0) & (c == 0) | (r == 1) & (c == 2), 1.0, 0.0)
    weights = jnp.where((r == 1) & (c == 1), 256.0, weights).astype(jnp.bfloat16)
    across = lax.dot_general(weights, queries[:, width:], NT, preferred_element_type=jnp.float32)
    down = members[:, width:].astype(jnp.float32)
    label_down = down[:, 0:1]
    order_down = down[:, 1:2] * 256.0 + down[:, 2:3]
    valid = (label_down == across[0:1, :]) & (order_down < across[1:2, :])
    best = jnp.max(jnp.where(valid, scores, -1.0), axis=0, keepdims=True)
    own, other = best[:, :size], best[:, size:]
    home = lax.broadcasted_iota(jnp.int32, (dests, size), 0)
    slot = lax.broadcasted_iota(jnp.int32, (dests, size), 1) // (size // dests)
    mine = home == slot
    out_ref[:dests, :] = jnp.where(mine, jnp.where(core == 0, own, other), -4.0)
    out_ref[dests:, :] = jnp.where(mine, jnp.where(core == 0, other, own), -4.0)


def pick_kernel(returned_ref, labels_ref, out_ref):
    lanes, size = returned_ref.shape[0] // 2, returned_ref.shape[1]
    _, hit, place = slots(labels_ref[...], lanes)
    cap = size // lanes
    lane = lax.rem(lax.broadcasted_iota(jnp.int32, (lanes, size), 1), cap)
    returned = jnp.maximum(returned_ref[:lanes, :], returned_ref[lanes:, :])
    best = jnp.full(hit.shape, -4.0, jnp.float32)
    for p in range(cap):
        value = jnp.max(jnp.where(lane == p, returned, -4.0), axis=1, keepdims=True)
        best = jnp.where(hit & (place == p), value, best)
    out_ref[...] = jnp.max(best, axis=0, keepdims=True)


def call(kernel, outs, specs, scratch=()):
    return pl.pallas_call(
        kernel,
        out_shape=outs,
        in_specs=specs,
        out_specs=jax.tree.map(lambda _: VMEM, outs),
        scratch_shapes=scratch,
        compiler_params=pltpu.CompilerParams(vmem_limit_bytes=16 * 1024 * 1024),
    )


def body(embeddings, labels, order):
    rows, width = embeddings.shape
    lanes = lax.axis_size(("x", "z"))
    cap = 2 * rows // lanes
    slot_count = lanes * cap
    wide = width + META
    labels, order = labels.reshape(1, rows), order.reshape(1, rows)

    core = lax.axis_index("core").astype(jnp.int32).reshape(1)
    sent = call(
        lambda *refs: pack_kernel(lanes, *refs),
        jax.ShapeDtypeStruct((slot_count, wide), jnp.bfloat16),
        [pl.BlockSpec(memory_space=pltpu.SMEM)] + [pl.BlockSpec(memory_space=pltpu.HBM)] * 3,
        [
            pltpu.VMEM((rows, width), jnp.bfloat16),
            pltpu.VMEM((1, rows), jnp.int32),
            pltpu.VMEM((1, rows), jnp.int32),
            pltpu.SemaphoreType.DMA((2 + DOWN * ACROSS,)),
        ],
    )(core, *[pltpu.with_memory_space_constraint(a, pltpu.HBM) for a in (embeddings, labels, order)])
    block = lax.all_to_all(sent.reshape(lanes, cap, wide), ("x", "z"), 0, 0, tiled=True)
    block = block.reshape(slot_count, wide)

    other = lax.ppermute(block, "core", [(0, 1), (1, 0)])
    copies = jnp.broadcast_to(block[None], (NY, slot_count, wide))
    lane = lax.all_to_all(copies, "y", 0, 0, tiled=True).reshape(NY * slot_count, wide)
    partial = call(
        gram_kernel,
        jax.ShapeDtypeStruct((2 * lanes, slot_count), jnp.float32),
        [pl.BlockSpec(memory_space=pltpu.SMEM)] + [VMEM] * 3,
    )(core, block, other, lane)
    returned = lax.all_to_all(
        partial.reshape(2 * lanes, 1, slot_count), ("core", "x", "z"), 0, 0, tiled=True
    )
    best = call(pick_kernel, jax.ShapeDtypeStruct((1, rows), jnp.float32), [VMEM] * 2)(
        returned.reshape(2 * lanes, slot_count), labels
    )
    return best.reshape(rows)


def solution(mesh):
    axes = ("y", "core", "x", "z")
    chips = Mesh(mesh.devices.reshape(NY, 2, NX, -1), axes)
    placed = (P(axes, None), P(axes), P(axes))
    return jax.shard_map(body, mesh=chips, in_specs=placed, out_specs=P(axes), check_vma=False)
```

```python
import jax
import jax.numpy as jnp
from jax import lax
from jax.experimental import pallas as pl
from jax.experimental.pallas import tpu as pltpu
from jax.sharding import Mesh
from jax.sharding import PartitionSpec as P

EPSILON = 1e-06
DOWN, ACROSS = 4, 4
SERIAL = 6
SHIFTS = (3, 1, 2)
NX = 4
NY = 4
META = 128
NT = (((1,), (1,)), ((), ()))
VMEM = pl.BlockSpec(memory_space=pltpu.VMEM)


def slots(labels, lanes):
    rows = labels.shape[1]
    target = lax.rem(labels, lanes)
    hit = lax.broadcasted_iota(jnp.int32, (lanes, rows), 0) == target
    earlier = lax.broadcasted_iota(jnp.int32, (rows, rows), 0) < lax.broadcasted_iota(jnp.int32, (rows, rows), 1)
    before = jnp.dot(
        hit.astype(jnp.bfloat16), earlier.astype(jnp.bfloat16), preferred_element_type=jnp.float32
    )
    place = jnp.sum(jnp.where(hit, before, 0.0), axis=0, keepdims=True).astype(jnp.int32)
    return target, hit, place


def pack_kernel(lanes, core_ref, emb_hbm, labels_hbm, order_hbm, out_ref, slot_ref, emb_ref, labels_ref, order_ref, arrived):
    rows, width = emb_ref.shape
    tall, wide = rows // DOWN, width // ACROSS
    pieces = [(pl.ds(r * tall, tall), pl.ds(c * wide, wide)) for r in range(DOWN) for c in range(ACROSS)]
    parts = [(labels_hbm, labels_ref), (order_hbm, order_ref)]
    parts += [(emb_hbm.at[piece], emb_ref.at[piece]) for piece in pieces]
    copies = [
        pltpu.make_async_copy(source, target, arrived.at[k]) for k, (source, target) in enumerate(parts)
    ]
    paced, others = copies[2 : 2 + SERIAL], copies[2 + SERIAL :]
    goes_first = core_ref[0] == 1
    for copy in copies[:2]:
        copy.start()
    for copy in paced:
        copy.start()

        @pl.when(jnp.logical_not(goes_first))
        def _():
            copy.wait()

    for copy in others:
        copy.start()

    slot_count = out_ref.shape[0]
    copies[0].wait()
    copies[1].wait()
    labels, order = labels_ref[...], order_ref[...]
    target, _, place = slots(labels, lanes)
    cap = slot_count // lanes
    slot = target * cap + place
    slot_ref[...] = slot
    here = lax.broadcasted_iota(jnp.int32, (slot_count, rows), 0) == slot

    def column(values):
        return jnp.sum(jnp.where(here, values.astype(jnp.float32), 0.0), axis=1, keepdims=True)

    lane = lax.broadcasted_iota(jnp.int32, (slot_count, META), 1)
    meta = jnp.where(lane == 0, column(labels // lanes + 1), 0.0)
    meta = jnp.where(lane == 1, column(order // 256), meta)
    meta = jnp.where(lane == 2, column(lax.rem(order, 256)), meta)
    out_ref[:, width:] = meta.astype(jnp.bfloat16)

    for copy in others:
        copy.wait()

    @pl.when(goes_first)
    def _():
        for copy in paced:
            copy.wait()

    floats = emb_ref[...].astype(jnp.float32)
    scale = lax.rsqrt(jnp.sum(floats * floats, axis=1, keepdims=True) + width * EPSILON)
    unit = (floats * scale).astype(jnp.bfloat16)
    out_ref[:, :width] = jnp.dot(
        here.astype(jnp.bfloat16), unit, preferred_element_type=jnp.float32
    ).astype(jnp.bfloat16)


def gram_kernel(core_ref, own_ref, other_ref, *rest):
    lane_refs, out_ref = rest[:-1], rest[-1]
    width = own_ref.shape[1] - META
    size = own_ref.shape[0]
    dests = out_ref.shape[0] // 2
    core = core_ref[0]
    queries = jnp.concatenate([own_ref[...], other_ref[...]], axis=0)
    members = jnp.concatenate([own_ref[...]] + [ref[...] for ref in lane_refs], axis=0)
    scores = lax.dot_general(
        members[:, :width], queries[:, :width], NT, preferred_element_type=jnp.float32
    )
    r = lax.broadcasted_iota(jnp.int32, (8, META), 0)
    c = lax.broadcasted_iota(jnp.int32, (8, META), 1)
    weights = jnp.where((r == 0) & (c == 0) | (r == 1) & (c == 2), 1.0, 0.0)
    weights = jnp.where((r == 1) & (c == 1), 256.0, weights).astype(jnp.bfloat16)
    across = lax.dot_general(weights, queries[:, width:], NT, preferred_element_type=jnp.float32)
    down = members[:, width:].astype(jnp.float32)
    label_down = down[:, 0:1]
    order_down = down[:, 1:2] * 256.0 + down[:, 2:3]
    valid = (label_down == across[0:1, :]) & (order_down < across[1:2, :])
    best = jnp.max(jnp.where(valid, scores, -1.0), axis=0, keepdims=True)
    own, other = best[:, :size], best[:, size:]
    home = lax.broadcasted_iota(jnp.int32, (dests, size), 0)
    slot = lax.broadcasted_iota(jnp.int32, (dests, size), 1) // (size // dests)
    mine = home == slot
    out_ref[:dests, :] = jnp.where(mine, jnp.where(core == 0, own, other), -4.0)
    out_ref[dests:, :] = jnp.where(mine, jnp.where(core == 0, other, own), -4.0)


def pick_kernel(returned_ref, slot_ref, out_ref):
    lanes, size = returned_ref.shape[0] // 2, returned_ref.shape[1]
    cap = size // lanes
    slot = slot_ref[...]
    owner = lax.broadcasted_iota(jnp.int32, (lanes, slot.shape[1]), 0) * cap
    lane = lax.rem(lax.broadcasted_iota(jnp.int32, (lanes, size), 1), cap)
    returned = jnp.maximum(returned_ref[:lanes, :], returned_ref[lanes:, :])
    best = jnp.full(owner.shape, -4.0, jnp.float32)
    for p in range(cap):
        value = jnp.max(jnp.where(lane == p, returned, -4.0), axis=1, keepdims=True)
        best = jnp.where(slot == owner + p, value, best)
    out_ref[...] = jnp.max(best, axis=0, keepdims=True)


def call(kernel, outs, specs, scratch=()):
    return pl.pallas_call(
        kernel,
        out_shape=outs,
        in_specs=specs,
        out_specs=jax.tree.map(lambda _: VMEM, outs),
        scratch_shapes=scratch,
        compiler_params=pltpu.CompilerParams(vmem_limit_bytes=16 * 1024 * 1024),
    )


def body(embeddings, labels, order):
    rows, width = embeddings.shape
    lanes = lax.axis_size(("x", "z"))
    cap = 2 * rows // lanes
    slot_count = lanes * cap
    wide = width + META
    labels, order = labels.reshape(1, rows), order.reshape(1, rows)

    core = lax.axis_index("core").astype(jnp.int32).reshape(1)
    sent, slot = call(
        lambda *refs: pack_kernel(lanes, *refs),
        [
            jax.ShapeDtypeStruct((slot_count, wide), jnp.bfloat16),
            jax.ShapeDtypeStruct((1, rows), jnp.int32),
        ],
        [pl.BlockSpec(memory_space=pltpu.SMEM)] + [pl.BlockSpec(memory_space=pltpu.HBM)] * 3,
        [
            pltpu.VMEM((rows, width), jnp.bfloat16),
            pltpu.VMEM((1, rows), jnp.int32),
            pltpu.VMEM((1, rows), jnp.int32),
            pltpu.SemaphoreType.DMA((2 + DOWN * ACROSS,)),
        ],
    )(core, *[pltpu.with_memory_space_constraint(a, pltpu.HBM) for a in (embeddings, labels, order)])
    block = lax.all_to_all(sent.reshape(lanes, cap, wide), ("x", "z"), 0, 0, tiled=True)
    block = block.reshape(slot_count, wide)

    lane = [
        lax.ppermute(block, "y", [(y, (y + shift) % NY) for y in range(NY)]) for shift in SHIFTS
    ]
    other = lax.ppermute(block, "core", [(0, 1), (1, 0)])
    partial = call(
        gram_kernel,
        jax.ShapeDtypeStruct((2 * lanes, slot_count), jnp.float32),
        [pl.BlockSpec(memory_space=pltpu.SMEM)] + [VMEM] * (1 + NY),
    )(core, block, other, *lane)
    returned = lax.all_to_all(
        partial.reshape(2 * lanes, 1, slot_count), ("core", "x", "z"), 0, 0, tiled=True
    )
    best = call(pick_kernel, jax.ShapeDtypeStruct((1, rows), jnp.float32), [VMEM] * 2)(
        returned.reshape(2 * lanes, slot_count), slot
    )
    return best.reshape(rows)


def solution(mesh):
    axes = ("y", "core", "x", "z")
    chips = Mesh(mesh.devices.reshape(NY, 2, NX, -1), axes)
    placed = (P(axes, None), P(axes), P(axes))
    return jax.shard_map(body, mesh=chips, in_specs=placed, out_specs=P(axes), check_vma=False)
```

```python
import jax
import jax.numpy as jnp
from jax import lax
from jax.experimental import pallas as pl
from jax.experimental.pallas import tpu as pltpu
from jax.sharding import Mesh
from jax.sharding import PartitionSpec as P

EPSILON = 1e-06
DOWN, ACROSS = 4, 4
SERIAL = 6
SHIFTS = (3, 1, 2)
NX = 4
NY = 4
META = 128
NT = (((1,), (1,)), ((), ()))
VMEM = pl.BlockSpec(memory_space=pltpu.VMEM)


def slots(labels, lanes):
    rows = labels.shape[1]
    target = lax.rem(labels, lanes)
    hit = lax.broadcasted_iota(jnp.int32, (lanes, rows), 0) == target
    earlier = lax.broadcasted_iota(jnp.int32, (rows, rows), 0) < lax.broadcasted_iota(jnp.int32, (rows, rows), 1)
    before = jnp.dot(
        hit.astype(jnp.bfloat16), earlier.astype(jnp.bfloat16), preferred_element_type=jnp.float32
    )
    place = jnp.sum(jnp.where(hit, before, 0.0), axis=0, keepdims=True).astype(jnp.int32)
    return target, hit, place


def pack_kernel(lanes, core_ref, emb_hbm, labels_hbm, order_hbm, out_ref, slot_ref, emb_ref, labels_ref, order_ref, arrived):
    rows, width = emb_ref.shape
    tall, wide = rows // DOWN, width // ACROSS
    pieces = [(pl.ds(r * tall, tall), pl.ds(c * wide, wide)) for r in range(DOWN) for c in range(ACROSS)]
    parts = [(labels_hbm, labels_ref), (order_hbm, order_ref)]
    parts += [(emb_hbm.at[piece], emb_ref.at[piece]) for piece in pieces]
    copies = [
        pltpu.make_async_copy(source, target, arrived.at[k]) for k, (source, target) in enumerate(parts)
    ]
    paced, others = copies[2 : 2 + SERIAL], copies[2 + SERIAL :]
    goes_first = core_ref[0] == 1
    for copy in copies[:2]:
        copy.start()
    for copy in paced:
        copy.start()

        @pl.when(jnp.logical_not(goes_first))
        def _():
            copy.wait()

    for copy in others:
        copy.start()

    slot_count = out_ref.shape[0]
    copies[0].wait()
    copies[1].wait()
    labels, order = labels_ref[...], order_ref[...]
    target, _, place = slots(labels, lanes)
    cap = slot_count // lanes
    slot = target * cap + place
    slot_ref[...] = slot
    here = lax.broadcasted_iota(jnp.int32, (slot_count, rows), 0) == slot

    def column(values):
        return jnp.sum(jnp.where(here, values.astype(jnp.float32), 0.0), axis=1, keepdims=True)

    lane = lax.broadcasted_iota(jnp.int32, (slot_count, META), 1)
    meta = jnp.where(lane == 0, column(labels // lanes + 1), 0.0)
    meta = jnp.where(lane == 1, column(order // 256), meta)
    meta = jnp.where(lane == 2, column(lax.rem(order, 256)), meta)
    out_ref[:, width:] = meta.astype(jnp.bfloat16)

    for copy in others:
        copy.wait()

    @pl.when(goes_first)
    def _():
        for copy in paced:
            copy.wait()

    floats = emb_ref[...].astype(jnp.float32)
    scale = lax.rsqrt(jnp.sum(floats * floats, axis=1, keepdims=True) + width * EPSILON)
    unit = (floats * scale).astype(jnp.bfloat16)
    out_ref[:, :width] = jnp.dot(
        here.astype(jnp.bfloat16), unit, preferred_element_type=jnp.float32
    ).astype(jnp.bfloat16)


def best_of(queries, member_refs):
    width = queries.shape[1] - META
    members = jnp.concatenate([ref[...] for ref in member_refs], axis=0)
    scores = lax.dot_general(
        members[:, :width], queries[:, :width], NT, preferred_element_type=jnp.float32
    )
    r = lax.broadcasted_iota(jnp.int32, (8, META), 0)
    c = lax.broadcasted_iota(jnp.int32, (8, META), 1)
    weights = jnp.where((r == 0) & (c == 0) | (r == 1) & (c == 2), 1.0, 0.0)
    weights = jnp.where((r == 1) & (c == 1), 256.0, weights).astype(jnp.bfloat16)
    across = lax.dot_general(weights, queries[:, width:], NT, preferred_element_type=jnp.float32)
    down = members[:, width:].astype(jnp.float32)
    label_down = down[:, 0:1]
    order_down = down[:, 1:2] * 256.0 + down[:, 2:3]
    valid = (label_down == across[0:1, :]) & (order_down < across[1:2, :])
    return jnp.max(jnp.where(valid, scores, -1.0), axis=0, keepdims=True)


def early_kernel(own_ref, *rest):
    rest[-1][...] = best_of(own_ref[...], (own_ref, *rest[:-1]))


def late_kernel(core_ref, early_ref, own_ref, other_ref, last_ref, *rest):
    lane_refs, out_ref = rest[:-1], rest[-1]
    size = own_ref.shape[0]
    dests = out_ref.shape[0] // 2
    core = core_ref[0]
    own = jnp.maximum(early_ref[...], best_of(own_ref[...], (last_ref,)))
    other = best_of(other_ref[...], (own_ref, last_ref, *lane_refs))
    home = lax.broadcasted_iota(jnp.int32, (dests, size), 0)
    slot = lax.broadcasted_iota(jnp.int32, (dests, size), 1) // (size // dests)
    mine = home == slot
    out_ref[:dests, :] = jnp.where(mine, jnp.where(core == 0, own, other), -4.0)
    out_ref[dests:, :] = jnp.where(mine, jnp.where(core == 0, other, own), -4.0)


def pick_kernel(returned_ref, slot_ref, out_ref):
    lanes, size = returned_ref.shape[0] // 2, returned_ref.shape[1]
    cap = size // lanes
    slot = slot_ref[...]
    owner = lax.broadcasted_iota(jnp.int32, (lanes, slot.shape[1]), 0) * cap
    lane = lax.rem(lax.broadcasted_iota(jnp.int32, (lanes, size), 1), cap)
    returned = jnp.maximum(returned_ref[:lanes, :], returned_ref[lanes:, :])
    best = jnp.full(owner.shape, -4.0, jnp.float32)
    for p in range(cap):
        value = jnp.max(jnp.where(lane == p, returned, -4.0), axis=1, keepdims=True)
        best = jnp.where(slot == owner + p, value, best)
    out_ref[...] = jnp.max(best, axis=0, keepdims=True)


def call(kernel, outs, specs, scratch=()):
    return pl.pallas_call(
        kernel,
        out_shape=outs,
        in_specs=specs,
        out_specs=jax.tree.map(lambda _: VMEM, outs),
        scratch_shapes=scratch,
        compiler_params=pltpu.CompilerParams(vmem_limit_bytes=16 * 1024 * 1024),
    )


def body(embeddings, labels, order):
    rows, width = embeddings.shape
    lanes = lax.axis_size(("x", "z"))
    cap = 2 * rows // lanes
    slot_count = lanes * cap
    wide = width + META
    labels, order = labels.reshape(1, rows), order.reshape(1, rows)

    core = lax.axis_index("core").astype(jnp.int32).reshape(1)
    sent, slot = call(
        lambda *refs: pack_kernel(lanes, *refs),
        [
            jax.ShapeDtypeStruct((slot_count, wide), jnp.bfloat16),
            jax.ShapeDtypeStruct((1, rows), jnp.int32),
        ],
        [pl.BlockSpec(memory_space=pltpu.SMEM)] + [pl.BlockSpec(memory_space=pltpu.HBM)] * 3,
        [
            pltpu.VMEM((rows, width), jnp.bfloat16),
            pltpu.VMEM((1, rows), jnp.int32),
            pltpu.VMEM((1, rows), jnp.int32),
            pltpu.SemaphoreType.DMA((2 + DOWN * ACROSS,)),
        ],
    )(core, *[pltpu.with_memory_space_constraint(a, pltpu.HBM) for a in (embeddings, labels, order)])
    block = lax.all_to_all(sent.reshape(lanes, cap, wide), ("x", "z"), 0, 0, tiled=True)
    block = block.reshape(slot_count, wide)

    lane = [
        lax.ppermute(block, "y", [(y, (y + shift) % NY) for y in range(NY)]) for shift in SHIFTS
    ]
    other = lax.ppermute(block, "core", [(0, 1), (1, 0)])
    last, ready = lane[0], [lane[1], lane[2]]
    early = call(early_kernel, jax.ShapeDtypeStruct((1, slot_count), jnp.float32), [VMEM] * 3)(
        block, *ready
    )
    partial = call(
        late_kernel,
        jax.ShapeDtypeStruct((2 * lanes, slot_count), jnp.float32),
        [pl.BlockSpec(memory_space=pltpu.SMEM)] + [VMEM] * 6,
    )(core, early, block, other, last, *ready)
    returned = lax.all_to_all(
        partial.reshape(2 * lanes, 1, slot_count), ("core", "x", "z"), 0, 0, tiled=True
    )
    best = call(pick_kernel, jax.ShapeDtypeStruct((1, rows), jnp.float32), [VMEM] * 2)(
        returned.reshape(2 * lanes, slot_count), slot
    )
    return best.reshape(rows)


def solution(mesh):
    axes = ("y", "core", "x", "z")
    chips = Mesh(mesh.devices.reshape(NY, 2, NX, -1), axes)
    placed = (P(axes, None), P(axes), P(axes))
    return jax.shard_map(body, mesh=chips, in_specs=placed, out_specs=P(axes), check_vma=False)
```

```python
import jax
import jax.numpy as jnp
from jax import lax
from jax.experimental import pallas as pl
from jax.experimental.pallas import tpu as pltpu
from jax.sharding import Mesh
from jax.sharding import PartitionSpec as P

EPSILON = 1e-06
DOWN, ACROSS = 4, 4
SERIAL = 6
SHIFTS = (3, 1, 2)
NX = 4
NY = 4
META = 128
NT = (((1,), (1,)), ((), ()))
VMEM = pl.BlockSpec(memory_space=pltpu.VMEM)


def slots(labels, lanes):
    rows = labels.shape[1]
    target = lax.rem(labels, lanes)
    hit = lax.broadcasted_iota(jnp.int32, (lanes, rows), 0) == target
    earlier = lax.broadcasted_iota(jnp.int32, (rows, rows), 0) < lax.broadcasted_iota(jnp.int32, (rows, rows), 1)
    before = jnp.dot(
        hit.astype(jnp.bfloat16), earlier.astype(jnp.bfloat16), preferred_element_type=jnp.float32
    )
    place = jnp.sum(jnp.where(hit, before, 0.0), axis=0, keepdims=True).astype(jnp.int32)
    return target, hit, place


def pack_kernel(lanes, core_ref, emb_hbm, labels_hbm, order_hbm, out_ref, slot_ref, emb_ref, labels_ref, order_ref, arrived):
    rows, width = emb_ref.shape
    tall, wide = rows // DOWN, width // ACROSS
    pieces = [(pl.ds(r * tall, tall), pl.ds(c * wide, wide)) for r in range(DOWN) for c in range(ACROSS)]
    parts = [(labels_hbm, labels_ref), (order_hbm, order_ref)]
    parts += [(emb_hbm.at[piece], emb_ref.at[piece]) for piece in pieces]
    copies = [
        pltpu.make_async_copy(source, target, arrived.at[k]) for k, (source, target) in enumerate(parts)
    ]
    paced, others = copies[2 : 2 + SERIAL], copies[2 + SERIAL :]
    goes_first = core_ref[0] == 1
    for copy in copies[:2]:
        copy.start()
    for copy in paced:
        copy.start()

        @pl.when(jnp.logical_not(goes_first))
        def _():
            copy.wait()

    for copy in others:
        copy.start()

    slot_count = out_ref.shape[0]
    copies[0].wait()
    copies[1].wait()
    labels, order = labels_ref[...], order_ref[...]
    target, _, place = slots(labels, lanes)
    cap = slot_count // lanes
    slot_ref[...] = target * cap + place
    nz = lanes // NX
    slot = (lax.rem(target, nz) * NX + target // nz) * cap + place
    here = lax.broadcasted_iota(jnp.int32, (slot_count, rows), 0) == slot

    def column(values):
        return jnp.sum(jnp.where(here, values.astype(jnp.float32), 0.0), axis=1, keepdims=True)

    lane = lax.broadcasted_iota(jnp.int32, (slot_count, META), 1)
    meta = jnp.where(lane == 0, column(labels // lanes + 1), 0.0)
    meta = jnp.where(lane == 1, column(order // 256), meta)
    meta = jnp.where(lane == 2, column(lax.rem(order, 256)), meta)
    out_ref[:, width:] = meta.astype(jnp.bfloat16)

    for copy in others:
        copy.wait()

    @pl.when(goes_first)
    def _():
        for copy in paced:
            copy.wait()

    floats = emb_ref[...].astype(jnp.float32)
    scale = lax.rsqrt(jnp.sum(floats * floats, axis=1, keepdims=True) + width * EPSILON)
    unit = (floats * scale).astype(jnp.bfloat16)
    out_ref[:, :width] = jnp.dot(
        here.astype(jnp.bfloat16), unit, preferred_element_type=jnp.float32
    ).astype(jnp.bfloat16)


def best_of(queries, member_refs):
    width = queries.shape[1] - META
    members = jnp.concatenate([ref[...] for ref in member_refs], axis=0)
    scores = lax.dot_general(
        members[:, :width], queries[:, :width], NT, preferred_element_type=jnp.float32
    )
    r = lax.broadcasted_iota(jnp.int32, (8, META), 0)
    c = lax.broadcasted_iota(jnp.int32, (8, META), 1)
    weights = jnp.where((r == 0) & (c == 0) | (r == 1) & (c == 2), 1.0, 0.0)
    weights = jnp.where((r == 1) & (c == 1), 256.0, weights).astype(jnp.bfloat16)
    across = lax.dot_general(weights, queries[:, width:], NT, preferred_element_type=jnp.float32)
    down = members[:, width:].astype(jnp.float32)
    label_down = down[:, 0:1]
    order_down = down[:, 1:2] * 256.0 + down[:, 2:3]
    valid = (label_down == across[0:1, :]) & (order_down < across[1:2, :])
    return jnp.max(jnp.where(valid, scores, -1.0), axis=0, keepdims=True)


def early_kernel(own_ref, *rest):
    rest[-1][...] = best_of(own_ref[...], (own_ref, *rest[:-1]))


def late_kernel(core_ref, early_ref, own_ref, other_ref, last_ref, *rest):
    lane_refs, out_ref = rest[:-1], rest[-1]
    size = own_ref.shape[0]
    dests = out_ref.shape[0] // 2
    core = core_ref[0]
    own = jnp.maximum(early_ref[...], best_of(own_ref[...], (last_ref,)))
    other = best_of(other_ref[...], (own_ref, last_ref, *lane_refs))
    home = lax.broadcasted_iota(jnp.int32, (dests, size), 0)
    slot = lax.broadcasted_iota(jnp.int32, (dests, size), 1) // (size // dests)
    slot = lax.rem(slot, NX) * (dests // NX) + slot // NX
    mine = home == slot
    out_ref[:dests, :] = jnp.where(mine, jnp.where(core == 0, own, other), -4.0)
    out_ref[dests:, :] = jnp.where(mine, jnp.where(core == 0, other, own), -4.0)


def pick_kernel(returned_ref, slot_ref, out_ref):
    lanes, size = returned_ref.shape[0] // 2, returned_ref.shape[1]
    cap = size // lanes
    slot = slot_ref[...]
    owner = lax.broadcasted_iota(jnp.int32, (lanes, slot.shape[1]), 0) * cap
    lane = lax.rem(lax.broadcasted_iota(jnp.int32, (lanes, size), 1), cap)
    returned = jnp.maximum(returned_ref[:lanes, :], returned_ref[lanes:, :])
    best = jnp.full(owner.shape, -4.0, jnp.float32)
    for p in range(cap):
        value = jnp.max(jnp.where(lane == p, returned, -4.0), axis=1, keepdims=True)
        best = jnp.where(slot == owner + p, value, best)
    out_ref[...] = jnp.max(best, axis=0, keepdims=True)


def call(kernel, outs, specs, scratch=()):
    return pl.pallas_call(
        kernel,
        out_shape=outs,
        in_specs=specs,
        out_specs=jax.tree.map(lambda _: VMEM, outs),
        scratch_shapes=scratch,
        compiler_params=pltpu.CompilerParams(vmem_limit_bytes=16 * 1024 * 1024),
    )


def body(embeddings, labels, order):
    rows, width = embeddings.shape
    lanes = lax.axis_size(("x", "z"))
    cap = 2 * rows // lanes
    slot_count = lanes * cap
    wide = width + META
    labels, order = labels.reshape(1, rows), order.reshape(1, rows)

    core = lax.axis_index("core").astype(jnp.int32).reshape(1)
    sent, slot = call(
        lambda *refs: pack_kernel(lanes, *refs),
        [
            jax.ShapeDtypeStruct((slot_count, wide), jnp.bfloat16),
            jax.ShapeDtypeStruct((1, rows), jnp.int32),
        ],
        [pl.BlockSpec(memory_space=pltpu.SMEM)] + [pl.BlockSpec(memory_space=pltpu.HBM)] * 3,
        [
            pltpu.VMEM((rows, width), jnp.bfloat16),
            pltpu.VMEM((1, rows), jnp.int32),
            pltpu.VMEM((1, rows), jnp.int32),
            pltpu.SemaphoreType.DMA((2 + DOWN * ACROSS,)),
        ],
    )(core, *[pltpu.with_memory_space_constraint(a, pltpu.HBM) for a in (embeddings, labels, order)])
    block = lax.all_to_all(sent.reshape(lanes, cap, wide), ("z", "x"), 0, 0, tiled=True)
    block = block.reshape(slot_count, wide)

    lane = [
        lax.ppermute(block, "y", [(y, (y + shift) % NY) for y in range(NY)]) for shift in SHIFTS
    ]
    other = lax.ppermute(block, "core", [(0, 1), (1, 0)])
    last, ready = lane[0], [lane[1], lane[2]]
    early = call(early_kernel, jax.ShapeDtypeStruct((1, slot_count), jnp.float32), [VMEM] * 3)(
        block, *ready
    )
    partial = call(
        late_kernel,
        jax.ShapeDtypeStruct((2 * lanes, slot_count), jnp.float32),
        [pl.BlockSpec(memory_space=pltpu.SMEM)] + [VMEM] * 6,
    )(core, early, block, other, last, *ready)
    returned = lax.all_to_all(
        partial.reshape(2 * lanes, 1, slot_count), ("core", "x", "z"), 0, 0, tiled=True
    )
    best = call(pick_kernel, jax.ShapeDtypeStruct((1, rows), jnp.float32), [VMEM] * 2)(
        returned.reshape(2 * lanes, slot_count), slot
    )
    return best.reshape(rows)


def solution(mesh):
    axes = ("y", "core", "x", "z")
    chips = Mesh(mesh.devices.reshape(NY, 2, NX, -1), axes)
    placed = (P(axes, None), P(axes), P(axes))
    return jax.shard_map(body, mesh=chips, in_specs=placed, out_specs=P(axes), check_vma=False)
```
